128 devices in a mesh: grp: 4 (over x_lo, core), scan: 32 (over z, y, x_hi).
Axes of the slice: x: 4 (x_hi: 2, x_lo: 2; x = x_hi * 2 + x_lo), y: 4, z: 4, core: 2. Of those that a mesh axis runs over, the one named last changes fastest.
Arguments:
- projection: float32 [8, 2, 256, 4096], P('grp', None, None, 'scan'), may hold values from -6 to 6
- illumination: float32 [2, 256, 256], replicated, may hold values from -6 to 6
- amplitude: float32 [8, 128, 256, 256], P('grp', 'scan'), may hold values from 0 to 2
- offsets: int32 [8, 128], P('grp', 'scan'), may hold values from -128 to 3968, as said below
Outputs:
- gradient: float32 [8, 2, 256, 4096], P(None, None, ('grp', 'scan'))
The draws below stay inside these ranges and needn't reach their ends.
Inputs may be any that keep to these rules, and one draw needn't show every extreme that they name: `offsets`: for every angle, scan position j has an offset between (j // 4) * 128 - 256 // 2 and that value plus 128; in each aligned block of 4 positions the first takes the lower end and the second the upper end.
All inputs are finite; a program needn't handle non-finite values.
Results may differ from the reference program's by a relative error of at most 0.0003.
Values sent between devices are 32-bit elements; how exact they have to be, the bound alone decides.
A program may use at most 64 MiB of HBM per device.

```python
import jax
import jax.numpy as jnp
from jax import lax

PATCH = 256
POS_DEV = 4
CD = 128
ROWS = 256
COLS = 4096
ANGLES = 8
POS = 128


def draw_offsets(key, part):
    spread = jax.random.randint(key, (ANGLES, POS), 0, CD + 1, dtype=jnp.int32)
    column = jnp.arange(POS, dtype=jnp.int32)
    within = column % POS_DEV
    spread = jnp.where(within[None, :] == 0, 0, jnp.where(within[None, :] == 1, CD, spread))
    return (column // POS_DEV * CD - PATCH // 2)[None, :] + spread


def steps_of(own_key, extent, split, low, top_value):
    def one(dim, shards_of):
        draws = jax.random.uniform(jax.random.fold_in(jax.random.fold_in(own_key, 6), dim), (shards_of,), jnp.float32, low / len(split), top_value / len(split))
        return jnp.repeat(jnp.exp(draws), extent[dim] // shards_of).reshape((-1,) + (1,) * (len(extent) - dim - 1))

    factor_of = one(*split[0])
    for cut in split[1:]:
        factor_of = factor_of * one(*cut)
    return factor_of


def gaussian(own_key, dims, deviation, reach, split=(), kind=jnp.bfloat16):
    factor_of = steps_of(own_key, dims, split, -0.22, 0.18) if split else 1.0
    drawn = jax.random.normal(own_key, dims, jnp.float32) * deviation * factor_of
    return jnp.minimum(jnp.maximum(drawn, -reach), reach).astype(kind)


def setup_inputs(seed: int = 0) -> dict:
    streams_of = jax.random.split(jax.random.key(seed), 5)
    return {
        "projection": gaussian(streams_of[0], (ANGLES, 2, ROWS, COLS), 0.7, 6.0, ((0, 4), (3, 32)), jnp.float32),
        "illumination": gaussian(streams_of[1], (2, PATCH, PATCH), 0.7, 6.0, (), jnp.float32),
        "amplitude": jnp.clip(2.0 * jax.random.uniform(streams_of[2], (ANGLES, POS, PATCH, PATCH), jnp.float32) ** steps_of(streams_of[2], (ANGLES, POS, PATCH, PATCH), ((0, 4), (1, 32)), -0.2, 0.2), 0.0, 2.0),
        "offsets": draw_offsets(jax.random.fold_in(streams_of[4], 71), 0),
    }


def reference(projection, illumination, amplitude, offsets):
    half_patch = PATCH // 2
    padded = jnp.pad(projection, ((0, 0), (0, 0), (0, 0), (half_patch, half_patch)))
    illum = lax.complex(illumination[0], illumination[1])

    def one_angle(packed):
        column_strip, angle_amp, angle_offsets = packed
        starts = (angle_offsets + half_patch).astype(jnp.int32)
        windows = jax.vmap(lambda start_col: lax.dynamic_slice_in_dim(column_strip, start_col, PATCH, 2))(starts)
        exit_wave = illum[None] * lax.complex(windows[:, 0], windows[:, 1])
        far_field = jnp.fft.fft2(exit_wave, norm="ortho")
        magnitude = jnp.abs(far_field)
        residual_field = far_field * (1.0 - angle_amp / jnp.maximum(magnitude, 0.5))
        back_field = jnp.fft.ifft2(residual_field, norm="ortho")
        patch_grad = jnp.conj(illum)[None] * back_field
        pairs = jnp.stack([jnp.real(patch_grad), jnp.imag(patch_grad)], axis=1)

        def add_patch(slot, summed):
            start_col = starts[slot]
            current = lax.dynamic_slice_in_dim(summed, start_col, PATCH, 2)
            return lax.dynamic_update_slice_in_dim(summed, current + pairs[slot], start_col, 2)

        summed = lax.fori_loop(0, POS, add_patch, jnp.zeros_like(column_strip))
        return summed[:, :, half_patch:half_patch + COLS]

    return lax.map(one_angle, (padded, amplitude, offsets))
```

```python
import functools
import math

import jax
import jax.numpy as jnp
import ml_dtypes
import numpy as np
from jax import lax
from jax.experimental import pallas as pl
from jax.experimental.pallas import tpu as pltpu
from jax.sharding import PartitionSpec as P

BF = jnp.bfloat16
F32 = jnp.float32
MESH = pl.DeviceIdType.MESH
GRP, SCAN = 4, 32
DEVS = GRP * SCAN
YZ = 16


def tables():
    n = np.arange(128)
    mats = []
    for odd in (0, 1):
        k = (np.arange(128) + 64 * odd) % 128
        angle = 2 * math.pi * ((n[None, :] * (2 * k[:, None] + odd)) % 256) / 256
        c, s = np.cos(angle) / 16, np.sin(angle) / 16
        forward = np.block([[c, s], [-s, c]])
        mats += [forward, forward.T]
    t = np.stack(mats)
    hi = t.astype(np.float32).astype(ml_dtypes.bfloat16)
    lo = (t - hi.astype(np.float64)).astype(np.float32).astype(ml_dtypes.bfloat16)
    return np.stack([hi, lo], 1)


def split(x):
    hi = x.astype(BF)
    return hi, (x - hi.astype(F32)).astype(BF)


def dot(a, b):
    return jnp.dot(a, b, preferred_element_type=F32)


def left(t_ref, i, x):
    hi, lo = split(x)
    return dot(t_ref[i, 0], hi) + dot(t_ref[i, 1], hi) + dot(t_ref[i, 0], lo)


def right(x, t_ref, i):
    hi, lo = split(x)
    return dot(hi, t_ref[i, 0]) + dot(lo, t_ref[i, 0]) + dot(hi, t_ref[i, 1])


def rolled_probe(ill_ref, d, c):
    lane = lax.broadcasted_iota(jnp.int32, (256, 128), 1)
    shift = lax.rem(d, 128)
    r0 = pltpu.roll(ill_ref[c, :, 0:128], shift, 1)
    r1 = pltpu.roll(ill_ref[c, :, 128:256], shift, 1)
    return jnp.where(lane < d, r0, r1), jnp.where(lane < d, r1, r0)


def ordered_amplitude(amp_ref, a, p):
    lane = lax.broadcasted_iota(jnp.int32, (128, 128), 1)
    first = lane < 64
    ia = jnp.where(first, 2 * lane, 2 * lane - 127)
    ib = jnp.where(first, 2 * lane + 1, 2 * lane - 128)
    even, odd = [], []
    for k in (0, 1):
        x = amp_ref[a, p, 0, pl.ds(k, 128, stride=2), :]
        y = amp_ref[a, p, 1, pl.ds(k, 128, stride=2), :]
        if k:
            x = jnp.concatenate([x[64:], x[:64]], 0)
            y = jnp.concatenate([y[64:], y[:64]], 0)
        x = jnp.take_along_axis(x, ia, axis=1, mode="promise_in_bounds")
        y = jnp.take_along_axis(y, ib, axis=1, mode="promise_in_bounds")
        even.append(jnp.where(first, x, y))
        odd.append(jnp.where(first, y, x))
    return jnp.concatenate(even, 0), jnp.concatenate(odd, 0)


def residual(f, amp):
    re, im = f[:, :128], f[:, 128:]
    w = 1.0 - amp * lax.rsqrt(jnp.maximum(re * re + im * im, 0.25))
    return jnp.concatenate([re * w, im * w], 1)


def patch(a, p, d, t_ref, ill_ref, amp_ref, tiles, acc):
    lane = lax.broadcasted_iota(jnp.int32, (256, 128), 1)
    m = lane < d
    ilr, irr = rolled_probe(ill_ref, d, 0)
    ili, iri = rolled_probe(ill_ref, d, 1)
    tl_r, tl_i = tiles[1, a, 0], tiles[1, a, 1]
    tr_r = jnp.where(m, tiles[2, a, 0], tiles[0, a, 0])
    tr_i = jnp.where(m, tiles[2, a, 1], tiles[0, a, 1])
    wr = jnp.concatenate([ilr * tl_r - ili * tl_i, irr * tr_r - iri * tr_i], 1)
    wi = jnp.concatenate([ilr * tl_i + ili * tl_r, irr * tr_i + iri * tr_r], 1)
    amp_even, amp_odd = ordered_amplitude(amp_ref, a, p)
    e = left(t_ref, 0, jnp.concatenate([wr[:128] + wr[128:], wi[:128] + wi[128:]], 0))
    o = left(t_ref, 2, jnp.concatenate([wr[:128] - wr[128:], wi[:128] - wi[128:]], 0))
    xr = jnp.concatenate([e[:128], o[:128]], 0)
    xi = jnp.concatenate([e[128:], o[128:]], 0)
    u = jnp.concatenate([xr[:, :128] + xr[:, 128:], xi[:, :128] + xi[:, 128:]], 1)
    v = jnp.concatenate([xr[:, :128] - xr[:, 128:], xi[:, :128] - xi[:, 128:]], 1)
    de = residual(right(u, t_ref, 1), amp_even)
    do = residual(right(v, t_ref, 3), amp_odd)
    be = right(de, t_ref, 0)
    bo = right(do, t_ref, 2)
    lh, rh = be + bo, be - bo
    yr = jnp.concatenate([lh[:, :128], rh[:, :128]], 1)
    yi = jnp.concatenate([lh[:, 128:], rh[:, 128:]], 1)
    e = left(t_ref, 1, jnp.concatenate([yr[:128], yi[:128]], 0))
    o = left(t_ref, 3, jnp.concatenate([yr[128:], yi[128:]], 0))
    top, bottom = e + o, e - o
    br = jnp.concatenate([top[:128], bottom[:128]], 0)
    bi = jnp.concatenate([top[128:], bottom[128:]], 0)
    acc[1, 0] += ilr * br[:, :128] + ili * bi[:, :128]
    acc[1, 1] += ilr * bi[:, :128] - ili * br[:, :128]
    gr_r = irr * br[:, 128:] + iri * bi[:, 128:]
    gr_i = irr * bi[:, 128:] - iri * br[:, 128:]
    acc[2, 0] += jnp.where(m, gr_r, 0.0)
    acc[2, 1] += jnp.where(m, gr_i, 0.0)
    acc[0, 0] += jnp.where(m, 0.0, gr_r)
    acc[0, 1] += jnp.where(m, 0.0, gr_i)


def kernel(
    off_ref, t_hbm, ill_hbm, amp_hbm, proj_hbm, out_ref,
    tab, ill, amp, tiles, acc, send, recv,
    local_sem, pair_send, pair_recv, fwd_send, fwd_recv, all_send, all_recv, own_sem, ready,
):
    g, s = lax.axis_index("grp"), lax.axis_index("scan")
    me = g * SCAN + s
    yz, odd = s // 2, s % 2
    local = [
        pltpu.make_async_copy(proj_hbm, tiles.at[1], local_sem.at[0]),
        pltpu.make_async_copy(ill_hbm, ill, local_sem.at[1]),
        pltpu.make_async_copy(t_hbm, tab, local_sem.at[2]),
        pltpu.make_async_copy(amp_hbm.at[:, :, :, pl.ds(0, 128)], amp.at[:, :, 0], local_sem.at[3]),
        pltpu.make_async_copy(amp_hbm.at[:, :, :, pl.ds(128, 128)], amp.at[:, :, 1], local_sem.at[4]),
    ]
    for c in local:
        c.start()

    barrier = pltpu.get_barrier_semaphore()
    row = g * 2 + odd
    for k in range(1, 8):
        other = (row + k) % 8
        pl.semaphore_signal(
            barrier, inc=1, device_id={"grp": other // 2, "scan": yz * 2 + other % 2}, device_id_type=MESH
        )
    for k in range(1, YZ):
        pl.semaphore_signal(
            barrier, inc=1, device_id={"grp": g, "scan": (yz + k) % YZ * 2 + odd}, device_id_type=MESH
        )
    pl.semaphore_wait(barrier, 7 + YZ - 1)

    near = 2 - 2 * odd
    local[0].wait()
    chunks = [(a, c) for a in range(2) for c in range(2)]

    def pair_copy(i):
        a, c = chunks[i]
        return pltpu.make_async_remote_copy(
            proj_hbm.at[a, c], tiles.at[2 * odd, a, c], pair_send.at[i], pair_recv.at[i],
            device_id={"grp": g, "scan": s + 1 - 2 * odd}, device_id_type=MESH,
        )

    def fwd_copy(i):
        a, c = chunks[i]
        return pltpu.make_async_remote_copy(
            tiles.at[near, a, c], tiles.at[2 * odd, a, c], fwd_send.at[i], fwd_recv.at[i],
            device_id={"grp": g, "scan": s + 2 - 4 * odd}, device_id_type=MESH,
        )

    for i in range(4):
        pair_copy(i).start()
    for k in range(1, YZ):
        pl.semaphore_signal(
            ready, inc=1, device_id={"grp": g, "scan": (yz + k) % YZ * 2 + odd}, device_id_type=MESH
        )
    sends_on = jnp.logical_and(s != SCAN - 2, s != 1)
    gets = jnp.logical_and(s != 0, s != SCAN - 1)

    @pl.when(jnp.logical_not(gets))
    def _():
        tiles[2 * odd] = jnp.zeros_like(tiles[0])

    for c in local[1:]:
        c.wait()

    def all_copy(a, k):
        to = (me + k) % DEVS
        return pltpu.make_async_remote_copy(
            send.at[a, to], recv.at[a, me], all_send.at[a], all_recv.at[a],
            device_id={"grp": to // SCAN, "scan": to % SCAN}, device_id_type=MESH,
        )

    for a in range(2):
        for i in (2 * a, 2 * a + 1):
            pair_copy(i).wait_recv()

            @pl.when(sends_on)
            def _():
                fwd_copy(i).start()

        for i in (2 * a, 2 * a + 1):

            @pl.when(gets)
            def _():
                fwd_copy(i).wait_recv()

        acc[...] = jnp.zeros_like(acc)

        def one(p, carry):
            patch(a, p, off_ref[a, p], tab, ill, amp, tiles, acc)
            return carry

        lax.fori_loop(0, 4, one, 0)

        def pack(q, carry):
            for u in range(4):
                to = q * 4 + u
                for t in range(3):
                    for c in range(2):
                        send[a, to, t, 2 * c : 2 * c + 2, :] = acc[t, c, pl.ds(to * 2, 2), :]
            return carry

        lax.fori_loop(0, DEVS // 4, pack, 0)
        if a == 0:
            pl.semaphore_wait(ready, YZ - 1)
        pltpu.make_async_copy(send.at[a, me], recv.at[a, me], own_sem.at[a]).start()

        def post(k, carry):
            all_copy(a, k).start()
            return carry

        lax.fori_loop(1, DEVS, post, 0)

    for i in range(4):
        pair_copy(i).wait_send()

        @pl.when(sends_on)
        def _():
            fwd_copy(i).wait_send()

    for a in range(2):
        pltpu.make_async_copy(send.at[a, me], recv.at[a, me], own_sem.at[a]).wait()
        bulk = pltpu.make_async_remote_copy(
            send.at[a, pl.ds(0, DEVS - 1)], recv.at[a, pl.ds(0, DEVS - 1)], all_send.at[a], all_recv.at[a],
            device_id={"grp": g, "scan": s + 1 - 2 * odd}, device_id_type=MESH,
        )
        bulk.wait_recv()

        def gather(h, carry):
            for t in range(SCAN):
                total = None
                for k in range(3):
                    src = t + 1 - k
                    if 0 <= src < SCAN:
                        x = recv[a, h * SCAN + src, k]
                        total = x if total is None else total + x
                for c in range(2):
                    out_ref[2 * h + a, c, :, 128 * t : 128 * t + 128] = total[2 * c : 2 * c + 2]
            return carry

        lax.fori_loop(0, GRP, gather, 0)
        bulk.wait_send()


def per_device(projection, illumination, amplitude, offsets):
    s = lax.axis_index("scan")
    d = offsets - (s * 128 - 128)
    return pl.pallas_call(
        kernel,
        out_shape=jax.ShapeDtypeStruct((8, 2, 2, 4096), F32),
        in_specs=[pl.BlockSpec(memory_space=pltpu.SMEM)] + [pl.BlockSpec(memory_space=pl.ANY)] * 4,
        out_specs=pl.BlockSpec(memory_space=pltpu.VMEM),
        scratch_shapes=[
            pltpu.VMEM((4, 2, 256, 256), BF),
            pltpu.VMEM((2, 256, 256), F32),
            pltpu.VMEM((2, 4, 2, 256, 128), F32),
            pltpu.VMEM((3, 2, 2, 256, 128), F32),
            pltpu.VMEM((3, 2, 256, 128), F32),
            pltpu.VMEM((2, DEVS, 3, 4, 128), F32),
            pltpu.VMEM((2, DEVS, 3, 4, 128), F32),
            pltpu.SemaphoreType.DMA((5,)),
            pltpu.SemaphoreType.DMA((4,)),
            pltpu.SemaphoreType.DMA((4,)),
            pltpu.SemaphoreType.DMA((4,)),
            pltpu.SemaphoreType.DMA((4,)),
            pltpu.SemaphoreType.DMA((2,)),
            pltpu.SemaphoreType.DMA((2,)),
            pltpu.SemaphoreType.DMA((2,)),
            pltpu.SemaphoreType.REGULAR,
        ],
        compiler_params=pltpu.CompilerParams(
            collective_id=0, has_side_effects=True, vmem_limit_bytes=48 << 20
        ),
        name="gradient",
    )(d, jnp.asarray(tables()), illumination, amplitude, projection)


def solution(mesh):
    placed = (P("grp", None, None, "scan"), P(), P("grp", "scan", None, None), P("grp", "scan"))
    return jax.shard_map(
        per_device,
        mesh=mesh,
        in_specs=placed,
        out_specs=P(None, None, ("grp", "scan"), None),
        check_vma=False,
    )
```

```python
import math

import jax
import jax.numpy as jnp
import ml_dtypes
import numpy as np
from jax import lax
from jax.experimental import pallas as pl
from jax.experimental.pallas import tpu as pltpu
from jax.sharding import PartitionSpec as P

BF = jnp.bfloat16
F32 = jnp.float32
MESH = pl.DeviceIdType.MESH
GRP, SCAN = 4, 32
DEVS = GRP * SCAN
YZ = 16
VMEM_LIMIT = 53 << 20


def tables():
    n = np.arange(128)
    mats = []
    for odd in (0, 1):
        k = (np.arange(128) + 64 * odd) % 128
        angle = 2 * math.pi * ((n[None, :] * (2 * k[:, None] + odd)) % 256) / 256
        c, s = np.cos(angle) / 16, np.sin(angle) / 16
        forward = np.block([[c, s], [-s, c]])
        mats += [forward, forward.T]
    t = np.stack(mats)
    hi = t.astype(np.float32).astype(ml_dtypes.bfloat16)
    lo = (t - hi.astype(np.float64)).astype(np.float32).astype(ml_dtypes.bfloat16)
    return np.stack([hi, lo], 1)


def split(x):
    hi = x.astype(BF)
    return hi, (x - hi.astype(F32)).astype(BF)


def dot(a, b):
    return jnp.dot(a, b, preferred_element_type=F32)


def left(t_ref, i, x):
    hi, lo = split(x)
    return dot(t_ref[i, 0], hi) + dot(t_ref[i, 1], hi) + dot(t_ref[i, 0], lo)


def right(x, t_ref, i):
    hi, lo = split(x)
    return dot(hi, t_ref[i, 0]) + dot(lo, t_ref[i, 0]) + dot(hi, t_ref[i, 1])


def cat(xs, axis):
    return jnp.concatenate(xs, axis)


def rows_forward(tab, wr, wi):
    e = left(tab, 0, cat([wr[:128] + wr[128:], wi[:128] + wi[128:]], 0))
    o = left(tab, 2, cat([wr[:128] - wr[128:], wi[:128] - wi[128:]], 0))
    return cat([e[:128], o[:128]], 0), cat([e[128:], o[128:]], 0)


def prepare(a, j, shift, tab, ill, amp, tiles, probe, ampo, near):
    lane = lax.broadcasted_iota(jnp.int32, (256, 128), 1)
    first = lane[:128] < 64
    ia = jnp.where(first, 2 * lane[:128], 2 * lane[:128] - 127)
    ib = jnp.where(first, 2 * lane[:128] + 1, 2 * lane[:128] - 128)
    waves = []
    for p2 in range(2):
        p = 2 * j + p2
        i = a * 4 + p
        d = shift(a, p)
        turn = lax.rem(d, 128)
        for c in range(2):
            r0 = pltpu.roll(ill[c, :, 0:128], turn, 1)
            r1 = pltpu.roll(ill[c, :, 128:256], turn, 1)
            probe[i, c] = jnp.where(lane < d, r0, r1)
            probe[i, 2 + c] = jnp.where(lane < d, r1, r0)
        pr, pi = probe[i, 0], probe[i, 1]
        tr, ti = tiles[1, a, 0], tiles[1, a, 1]
        waves.append((pr * tr - pi * ti, pr * ti + pi * tr))
        for k in (0, 1):
            x = amp[a, p, 0, pl.ds(k, 128, stride=2), :]
            y = amp[a, p, 1, pl.ds(k, 128, stride=2), :]
            if k:
                x = cat([x[64:], x[:64]], 0)
                y = cat([y[64:], y[:64]], 0)
            x = jnp.take_along_axis(x, ia, axis=1, mode="promise_in_bounds")
            y = jnp.take_along_axis(y, ib, axis=1, mode="promise_in_bounds")
            ampo[i, 0, 128 * k : 128 * k + 128] = jnp.where(first, x, y)
            ampo[i, 1, 128 * k : 128 * k + 128] = jnp.where(first, y, x)
    fr, fi = rows_forward(tab, cat([waves[0][0], waves[1][0]], 1), cat([waves[0][1], waves[1][1]], 1))
    for p2 in range(2):
        i = a * 4 + 2 * j + p2
        near[i, 0] = fr[:, 128 * p2 : 128 * p2 + 128]
        near[i, 1] = fi[:, 128 * p2 : 128 * p2 + 128]


def residual(f, amp):
    re, im = f[:, :128], f[:, 128:]
    w = 1.0 - amp * lax.rsqrt(jnp.maximum(re * re + im * im, 0.25))
    return cat([re * w, im * w], 1)


def finish(a, j, shift, tab, tiles, probe, ampo, near, acc):
    lane = lax.broadcasted_iota(jnp.int32, (256, 128), 1)
    waves, masks, backs = [], [], []
    for p2 in range(2):
        i = a * 4 + 2 * j + p2
        m = lane < shift(a, 2 * j + p2)
        masks.append(m)
        pr, pi = probe[i, 2], probe[i, 3]
        tr = jnp.where(m, tiles[2, a, 0], tiles[0, a, 0])
        ti = jnp.where(m, tiles[2, a, 1], tiles[0, a, 1])
        waves.append((pr * tr - pi * ti, pr * ti + pi * tr))
    fr, fi = rows_forward(tab, cat([waves[0][0], waves[1][0]], 1), cat([waves[0][1], waves[1][1]], 1))
    for p2 in range(2):
        i = a * 4 + 2 * j + p2
        ar, ai = near[i, 0], near[i, 1]
        br, bi = fr[:, 128 * p2 : 128 * p2 + 128], fi[:, 128 * p2 : 128 * p2 + 128]
        fe = right(cat([ar + br, ai + bi], 1), tab, 1)
        fo = right(cat([ar - br, ai - bi], 1), tab, 3)
        backs.append((right(residual(fe, ampo[i, 0]), tab, 0), right(residual(fo, ampo[i, 1]), tab, 2)))
    sums = None
    for p2 in range(2):
        i = a * 4 + 2 * j + p2
        m = masks[p2]
        be, bo = backs[p2]
        lh, rh = be + bo, be - bo
        yr = cat([lh[:, :128], rh[:, :128]], 1)
        yi = cat([lh[:, 128:], rh[:, 128:]], 1)
        e = left(tab, 1, cat([yr[:128], yi[:128]], 0))
        o = left(tab, 3, cat([yr[128:], yi[128:]], 0))
        top, bottom = e + o, e - o
        br = cat([top[:128], bottom[:128]], 0)
        bi = cat([top[128:], bottom[128:]], 0)
        pr, pi, qr, qi = probe[i, 0], probe[i, 1], probe[i, 2], probe[i, 3]
        gr = qr * br[:, 128:] + qi * bi[:, 128:]
        gi = qr * bi[:, 128:] - qi * br[:, 128:]
        parts = [
            jnp.where(m, 0.0, gr), jnp.where(m, 0.0, gi),
            pr * br[:, :128] + pi * bi[:, :128], pr * bi[:, :128] - pi * br[:, :128],
            jnp.where(m, gr, 0.0), jnp.where(m, gi, 0.0),
        ]
        sums = parts if sums is None else [x + y for x, y in zip(sums, parts)]
    for q in range(6):
        acc[a, q // 2, q % 2] += sums[q]


def kernel(
    off_hbm, t_hbm, ill_hbm, amp_hbm, proj_hbm, out_ref,
    off_ref, tab, ill, amp, tiles, probe, ampo, near, acc, send, recv,
    local_sem, pair_send, pair_recv, fwd_send, fwd_recv, all_send, all_recv, own_sem, ready,
):
    g, s = lax.axis_index("grp"), lax.axis_index("scan")
    me = g * SCAN + s
    yz, odd = s // 2, s % 2
    local = [
        pltpu.make_async_copy(proj_hbm, tiles.at[1], local_sem.at[0]),
        pltpu.make_async_copy(ill_hbm, ill, local_sem.at[1]),
        pltpu.make_async_copy(t_hbm, tab, local_sem.at[2]),
        pltpu.make_async_copy(amp_hbm.at[:, :, :, pl.ds(0, 128)], amp.at[:, :, 0], local_sem.at[3]),
        pltpu.make_async_copy(amp_hbm.at[:, :, :, pl.ds(128, 128)], amp.at[:, :, 1], local_sem.at[4]),
        pltpu.make_async_copy(off_hbm, off_ref, local_sem.at[5]),
    ]
    barrier = pltpu.get_barrier_semaphore()
    row = g * 2 + odd
    for k in range(1, 8):
        other = (row + k) % 8
        pl.semaphore_signal(
            barrier, inc=1, device_id={"grp": other // 2, "scan": yz * 2 + other % 2}, device_id_type=MESH
        )
    for k in range(1, YZ):
        pl.semaphore_signal(
            barrier, inc=1, device_id={"grp": g, "scan": (yz + k) % YZ * 2 + odd}, device_id_type=MESH
        )
    for c in local:
        c.start()
    acc[...] = jnp.zeros_like(acc)
    sends_on = jnp.logical_and(s != SCAN - 2, s != 1)
    gets = jnp.logical_and(s != 0, s != SCAN - 1)

    @pl.when(jnp.logical_not(gets))
    def _():
        tiles[2 * odd] = jnp.zeros_like(tiles[0])

    pl.semaphore_wait(barrier, 7 + YZ - 1)

    near_slot = 2 - 2 * odd
    chunks = [(a, c, h) for a in range(2) for c in range(2) for h in range(2)]

    def pair_copy(i):
        a, c, h = chunks[i]
        rows = pl.ds(128 * h, 128)
        return pltpu.make_async_remote_copy(
            proj_hbm.at[a, c, rows], tiles.at[2 * odd, a, c, rows], pair_send.at[i], pair_recv.at[i],
            device_id={"grp": g, "scan": s + 1 - 2 * odd}, device_id_type=MESH,
        )

    def fwd_copy(i):
        a, c, h = chunks[i]
        rows = pl.ds(128 * h, 128)
        return pltpu.make_async_remote_copy(
            tiles.at[near_slot, a, c, rows], tiles.at[2 * odd, a, c, rows], fwd_send.at[i], fwd_recv.at[i],
            device_id={"grp": g, "scan": s + 2 - 4 * odd}, device_id_type=MESH,
        )

    def pass_on(i):
        pair_copy(i).wait_recv()

        @pl.when(sends_on)
        def _():
            fwd_copy(i).start()

    def all_copy(a, k):
        to = (me + k) % DEVS
        return pltpu.make_async_remote_copy(
            send.at[a, to], recv.at[a, me], all_send.at[a], all_recv.at[a],
            device_id={"grp": to // SCAN, "scan": to % SCAN}, device_id_type=MESH,
        )

    def shift(a, p):
        return off_ref[a, p] - (s * 128 - 128)

    for i in range(4):
        pair_copy(i).start()
    for k in range(1, YZ):
        pl.semaphore_signal(
            ready, inc=1, device_id={"grp": g, "scan": (yz + k) % YZ * 2 + odd}, device_id_type=MESH
        )
    for c in local:
        c.wait()
    for q in range(4):
        prepare(q // 2, q % 2, shift, tab, ill, amp, tiles, probe, ampo, near)
        pass_on(q)
        pair_copy(q).wait_send()
        pair_copy(q + 4).start()

    for a in range(2):

        @pl.when(gets)
        def _():
            for i in range(4 * a, 4 * a + 4):
                fwd_copy(i).wait_recv()

        for j in range(2):
            if a == 0:
                pass_on(4 + 2 * j)
                pass_on(5 + 2 * j)
            finish(a, j, shift, tab, tiles, probe, ampo, near, acc)

        def pack(q, carry):
            for u in range(4):
                to = q * 4 + u
                for t in range(3):
                    for c in range(2):
                        send[a, to, t, 2 * c : 2 * c + 2, :] = acc[a, t, c, pl.ds(to * 2, 2), :]
            return carry

        lax.fori_loop(0, DEVS // 4, pack, 0)
        if a == 0:
            pl.semaphore_wait(ready, YZ - 1)

        def post(k, carry):
            all_copy(a, k).start()
            return carry

        lax.fori_loop(1, DEVS, post, 0)
        pltpu.make_async_copy(send.at[a, me], recv.at[a, me], own_sem.at[a]).start()

    for i in range(8):
        if i >= 4:
            pair_copy(i).wait_send()

        @pl.when(sends_on)
        def _():
            fwd_copy(i).wait_send()

    for a in range(2):
        pltpu.make_async_copy(send.at[a, me], recv.at[a, me], own_sem.at[a]).wait()
        bulk = pltpu.make_async_remote_copy(
            send.at[a, pl.ds(0, DEVS - 1)], recv.at[a, pl.ds(0, DEVS - 1)], all_send.at[a], all_recv.at[a],
            device_id={"grp": g, "scan": s + 1 - 2 * odd}, device_id_type=MESH,
        )
        bulk.wait_recv()

        def gather(h, carry):
            for t in range(SCAN):
                total = None
                for k in range(3):
                    src = t + 1 - k
                    if 0 <= src < SCAN:
                        x = recv[a, h * SCAN + src, k]
                        total = x if total is None else total + x
                for c in range(2):
                    out_ref[2 * h + a, c, :, 128 * t : 128 * t + 128] = total[2 * c : 2 * c + 2]
            return carry

        lax.fori_loop(0, GRP, gather, 0)
        bulk.wait_send()


def per_device(projection, illumination, amplitude, offsets):
    return pl.pallas_call(
        kernel,
        out_shape=jax.ShapeDtypeStruct((8, 2, 2, 4096), F32),
        in_specs=[pl.BlockSpec(memory_space=pl.ANY)] * 5,
        out_specs=pl.BlockSpec(memory_space=pltpu.VMEM),
        scratch_shapes=[
            pltpu.SMEM((2, 4), jnp.int32),
            pltpu.VMEM((4, 2, 256, 256), BF),
            pltpu.VMEM((2, 256, 256), F32),
            pltpu.VMEM((2, 4, 2, 256, 128), F32),
            pltpu.VMEM((3, 2, 2, 256, 128), F32),
            pltpu.VMEM((8, 4, 256, 128), F32),
            pltpu.VMEM((8, 2, 256, 128), F32),
            pltpu.VMEM((8, 2, 256, 128), F32),
            pltpu.VMEM((2, 3, 2, 256, 128), F32),
            pltpu.VMEM((2, DEVS, 3, 4, 128), F32),
            pltpu.VMEM((2, DEVS, 3, 4, 128), F32),
            pltpu.SemaphoreType.DMA((6,)),
            pltpu.SemaphoreType.DMA((8,)),
            pltpu.SemaphoreType.DMA((8,)),
            pltpu.SemaphoreType.DMA((8,)),
            pltpu.SemaphoreType.DMA((8,)),
            pltpu.SemaphoreType.DMA((2,)),
            pltpu.SemaphoreType.DMA((2,)),
            pltpu.SemaphoreType.DMA((2,)),
            pltpu.SemaphoreType.REGULAR,
        ],
        compiler_params=pltpu.CompilerParams(
            collective_id=0, has_side_effects=True, vmem_limit_bytes=VMEM_LIMIT
        ),
        name="gradient",
    )(offsets, jnp.asarray(tables()), illumination, amplitude, projection)


def solution(mesh):
    placed = (P("grp", None, None, "scan"), P(), P("grp", "scan", None, None), P("grp", "scan"))
    return jax.shard_map(
        per_device,
        mesh=mesh,
        in_specs=placed,
        out_specs=P(None, None, ("grp", "scan"), None),
        check_vma=False,
    )
```

```python
import math

import jax
import jax.numpy as jnp
import ml_dtypes
import numpy as np
from jax import lax
from jax.experimental import pallas as pl
from jax.experimental.pallas import tpu as pltpu
from jax.sharding import PartitionSpec as P

BF = jnp.bfloat16
F32 = jnp.float32
MESH = pl.DeviceIdType.MESH
GRP, SCAN = 4, 32
DEVS = GRP * SCAN
YZ = 16
BETWEEN = 1
VMEM_LIMIT = 53 << 20


def tables():
    n = np.arange(128)
    mats = []
    for odd in (0, 1):
        k = (np.arange(128) + 64 * odd) % 128
        angle = 2 * math.pi * ((n[None, :] * (2 * k[:, None] + odd)) % 256) / 256
        c, s = np.cos(angle) / 16, np.sin(angle) / 16
        forward = np.block([[c, s], [-s, c]])
        mats += [forward, forward.T]
    t = np.stack(mats)
    hi = t.astype(np.float32).astype(ml_dtypes.bfloat16)
    lo = (t - hi.astype(np.float64)).astype(np.float32).astype(ml_dtypes.bfloat16)
    return np.stack([hi, lo], 1)


def split(x):
    hi = x.astype(BF)
    return hi, (x - hi.astype(F32)).astype(BF)


def dot(a, b):
    return jnp.dot(a, b, preferred_element_type=F32)


def left(t_ref, i, x):
    hi, lo = split(x)
    return dot(t_ref[i, 0], hi) + dot(t_ref[i, 1], hi) + dot(t_ref[i, 0], lo)


def right(x, t_ref, i):
    hi, lo = split(x)
    return dot(hi, t_ref[i, 0]) + dot(lo, t_ref[i, 0]) + dot(hi, t_ref[i, 1])


def cat(xs, axis):
    return jnp.concatenate(xs, axis)


def rows_forward(tab, wr, wi):
    e = left(tab, 0, cat([wr[:128] + wr[128:], wi[:128] + wi[128:]], 0))
    o = left(tab, 2, cat([wr[:128] - wr[128:], wi[:128] - wi[128:]], 0))
    return cat([e[:128], o[:128]], 0), cat([e[128:], o[128:]], 0)


def prepare(a, j, shift, tab, ill, amp, tiles, probe, ampo, near):
    lane = lax.broadcasted_iota(jnp.int32, (256, 128), 1)
    first = lane[:128] < 64
    ia = jnp.where(first, 2 * lane[:128], 2 * lane[:128] - 127)
    ib = jnp.where(first, 2 * lane[:128] + 1, 2 * lane[:128] - 128)
    waves = []
    for p2 in range(2):
        p = 2 * j + p2
        i = a * 4 + p
        d = shift(a, p)
        turn = lax.rem(d, 128)
        for c in range(2):
            r0 = pltpu.roll(ill[c, :, 0:128], turn, 1)
            r1 = pltpu.roll(ill[c, :, 128:256], turn, 1)
            probe[i, c] = jnp.where(lane < d, r0, r1)
            probe[i, 2 + c] = jnp.where(lane < d, r1, r0)
        pr, pi = probe[i, 0], probe[i, 1]
        tr, ti = tiles[1, a, 0], tiles[1, a, 1]
        waves.append((pr * tr - pi * ti, pr * ti + pi * tr))
        for k in (0, 1):
            x = amp[a, p, 0, pl.ds(k, 128, stride=2), :]
            y = amp[a, p, 1, pl.ds(k, 128, stride=2), :]
            if k:
                x = cat([x[64:], x[:64]], 0)
                y = cat([y[64:], y[:64]], 0)
            x = jnp.take_along_axis(x, ia, axis=1, mode="promise_in_bounds")
            y = jnp.take_along_axis(y, ib, axis=1, mode="promise_in_bounds")
            ampo[i, 0, 128 * k : 128 * k + 128] = jnp.where(first, x, y)
            ampo[i, 1, 128 * k : 128 * k + 128] = jnp.where(first, y, x)
    fr, fi = rows_forward(tab, cat([waves[0][0], waves[1][0]], 1), cat([waves[0][1], waves[1][1]], 1))
    for p2 in range(2):
        i = a * 4 + 2 * j + p2
        near[i, 0] = fr[:, 128 * p2 : 128 * p2 + 128]
        near[i, 1] = fi[:, 128 * p2 : 128 * p2 + 128]


def residual(f, amp):
    re, im = f[:, :128], f[:, 128:]
    w = 1.0 - amp * lax.rsqrt(jnp.maximum(re * re + im * im, 0.25))
    return cat([re * w, im * w], 1)


def finish(a, ps, shift, tab, tiles, probe, ampo, near, acc, between=None):
    lane = lax.broadcasted_iota(jnp.int32, (256, 128), 1)
    index = [a * 4 + p for p in ps]
    masks = [lane < shift(a, p) for p in ps]
    waves = []
    for i, m in zip(index, masks):
        pr, pi = probe[i, 2], probe[i, 3]
        tr = jnp.where(m, tiles[2, a, 0], tiles[0, a, 0])
        ti = jnp.where(m, tiles[2, a, 1], tiles[0, a, 1])
        waves.append((pr * tr - pi * ti, pr * ti + pi * tr))
    far = []
    for q in range(0, len(ps), 2):
        pair = waves[q : q + 2]
        fr, fi = rows_forward(tab, cat([w[0] for w in pair], 1), cat([w[1] for w in pair], 1))
        for u in range(len(pair)):
            far.append((fr[:, 128 * u : 128 * u + 128], fi[:, 128 * u : 128 * u + 128]))
    fields = []
    for i, (br, bi) in zip(index, far):
        ar, ai = near[i, 0], near[i, 1]
        fields.append((right(cat([ar + br, ai + bi], 1), tab, 1), right(cat([ar - br, ai - bi], 1), tab, 3)))
    if between is not None:
        between(0)
    backs = []
    for i, (fe, fo) in zip(index, fields):
        backs.append((right(residual(fe, ampo[i, 0]), tab, 0), right(residual(fo, ampo[i, 1]), tab, 2)))
    if between is not None:
        between(1)
    rows = []
    for be, bo in backs:
        lh, rh = be + bo, be - bo
        yr = cat([lh[:, :128], rh[:, :128]], 1)
        yi = cat([lh[:, 128:], rh[:, 128:]], 1)
        rows.append((left(tab, 1, cat([yr[:128], yi[:128]], 0)), left(tab, 3, cat([yr[128:], yi[128:]], 0))))
    sums = None
    for i, m, (e, o) in zip(index, masks, rows):
        top, bottom = e + o, e - o
        br = cat([top[:128], bottom[:128]], 0)
        bi = cat([top[128:], bottom[128:]], 0)
        pr, pi, qr, qi = probe[i, 0], probe[i, 1], probe[i, 2], probe[i, 3]
        gr = qr * br[:, 128:] + qi * bi[:, 128:]
        gi = qr * bi[:, 128:] - qi * br[:, 128:]
        parts = [
            jnp.where(m, 0.0, gr), jnp.where(m, 0.0, gi),
            pr * br[:, :128] + pi * bi[:, :128], pr * bi[:, :128] - pi * br[:, :128],
            jnp.where(m, gr, 0.0), jnp.where(m, gi, 0.0),
        ]
        sums = parts if sums is None else [x + y for x, y in zip(sums, parts)]
    for q in range(6):
        acc[a, q // 2, q % 2] += sums[q]


def kernel(
    off_hbm, t_hbm, ill_hbm, amp_hbm, proj_hbm, out_ref,
    off_ref, tab, ill, amp, tiles, probe, ampo, near, acc, send, recv,
    local_sem, pair_send, pair_recv, fwd_send, fwd_recv, all_send, all_recv, own_sem, ready,
):
    g, s = lax.axis_index("grp"), lax.axis_index("scan")
    me = g * SCAN + s
    yz, odd = s // 2, s % 2
    local = [
        pltpu.make_async_copy(proj_hbm, tiles.at[1], local_sem.at[0]),
        pltpu.make_async_copy(ill_hbm, ill, local_sem.at[1]),
        pltpu.make_async_copy(t_hbm, tab, local_sem.at[2]),
        pltpu.make_async_copy(amp_hbm.at[:, :, :, pl.ds(0, 128)], amp.at[:, :, 0], local_sem.at[3]),
        pltpu.make_async_copy(amp_hbm.at[:, :, :, pl.ds(128, 128)], amp.at[:, :, 1], local_sem.at[4]),
        pltpu.make_async_copy(off_hbm, off_ref, local_sem.at[5]),
    ]
    barrier = pltpu.get_barrier_semaphore()
    row = g * 2 + odd
    for k in range(1, 8):
        other = (row + k) % 8
        pl.semaphore_signal(
            barrier, inc=1, device_id={"grp": other // 2, "scan": yz * 2 + other % 2}, device_id_type=MESH
        )
    for k in range(1, YZ):
        pl.semaphore_signal(
            barrier, inc=1, device_id={"grp": g, "scan": (yz + k) % YZ * 2 + odd}, device_id_type=MESH
        )
    for c in local:
        c.start()
    acc[...] = jnp.zeros_like(acc)
    sends_on = jnp.logical_and(s != SCAN - 2, s != 1)
    gets = jnp.logical_and(s != 0, s != SCAN - 1)

    @pl.when(jnp.logical_not(gets))
    def _():
        tiles[2 * odd] = jnp.zeros_like(tiles[0])

    pl.semaphore_wait(barrier, 7 + YZ - 1)

    near_slot = 2 - 2 * odd
    chunks = [(a, c, h) for a in range(2) for c in range(2) for h in range(2)]

    def pair_copy(i):
        a, c, h = chunks[i]
        rows = pl.ds(128 * h, 128)
        return pltpu.make_async_remote_copy(
            proj_hbm.at[a, c, rows], tiles.at[2 * odd, a, c, rows], pair_send.at[i], pair_recv.at[i],
            device_id={"grp": g, "scan": s + 1 - 2 * odd}, device_id_type=MESH,
        )

    def fwd_copy(i):
        a, c, h = chunks[i]
        rows = pl.ds(128 * h, 128)
        return pltpu.make_async_remote_copy(
            tiles.at[near_slot, a, c, rows], tiles.at[2 * odd, a, c, rows], fwd_send.at[i], fwd_recv.at[i],
            device_id={"grp": g, "scan": s + 2 - 4 * odd}, device_id_type=MESH,
        )

    def pass_on(i):
        pair_copy(i).wait_recv()

        @pl.when(sends_on)
        def _():
            fwd_copy(i).start()

    def all_copy(a, k):
        to = (me + k) % DEVS
        return pltpu.make_async_remote_copy(
            send.at[a, to], recv.at[a, me], all_send.at[a], all_recv.at[a],
            device_id={"grp": to // SCAN, "scan": to % SCAN}, device_id_type=MESH,
        )

    def shift(a, p):
        return off_ref[a, p] - (s * 128 - 128)

    for i in range(4):
        pair_copy(i).start()
    for k in range(1, YZ):
        pl.semaphore_signal(
            ready, inc=1, device_id={"grp": g, "scan": (yz + k) % YZ * 2 + odd}, device_id_type=MESH
        )
    for c in local:
        c.wait()
    for q in range(4):
        prepare(q // 2, q % 2, shift, tab, ill, amp, tiles, probe, ampo, near)
        pass_on(q)
        pair_copy(q).wait_send()
        pair_copy(q + 4).start()

    soon = 1 - odd
    later = [odd, 2, 3]

    def forwarded(a):
        @pl.when(gets)
        def _():
            for i in range(4 * a, 4 * a + 4):
                fwd_copy(i).wait_recv()

    for a in range(2):
        if a == 0:
            pass_on(4)
            pass_on(5)
            pass_on(6)
            forwarded(0)
            finish(a, [0, 1, 2, 3], shift, tab, tiles, probe, ampo, near, acc)
            pass_on(7)
        else:
            forwarded(1)
            finish(a, [0, 1, 2, 3], shift, tab, tiles, probe, ampo, near, acc)

        def pack(q, carry):
            for u in range(4):
                to = q * 4 + u
                for t in range(3):
                    for c in range(2):
                        send[a, to, t, 2 * c : 2 * c + 2, :] = acc[a, t, c, pl.ds(to * 2, 2), :]
            return carry

        lax.fori_loop(0, DEVS // 4, pack, 0)
        if a == 0:
            pl.semaphore_wait(ready, YZ - 1)

        def post(k, carry):
            all_copy(a, k).start()
            return carry

        lax.fori_loop(1, DEVS, post, 0)
        pltpu.make_async_copy(send.at[a, me], recv.at[a, me], own_sem.at[a]).start()

    for i in range(8):
        if i >= 4:
            pair_copy(i).wait_send()

        @pl.when(sends_on)
        def _():
            fwd_copy(i).wait_send()

    for a in range(2):
        pltpu.make_async_copy(send.at[a, me], recv.at[a, me], own_sem.at[a]).wait()
        bulk = pltpu.make_async_remote_copy(
            send.at[a, pl.ds(0, DEVS - 1)], recv.at[a, pl.ds(0, DEVS - 1)], all_send.at[a], all_recv.at[a],
            device_id={"grp": g, "scan": s + 1 - 2 * odd}, device_id_type=MESH,
        )
        bulk.wait_recv()

        def gather(h, carry):
            for t in range(SCAN):
                total = None
                for k in range(3):
                    src = t + 1 - k
                    if 0 <= src < SCAN:
                        x = recv[a, h * SCAN + src, k]
                        total = x if total is None else total + x
                for c in range(2):
                    out_ref[2 * h + a, c, :, 128 * t : 128 * t + 128] = total[2 * c : 2 * c + 2]
            return carry

        lax.fori_loop(0, GRP, gather, 0)
        bulk.wait_send()


def per_device(projection, illumination, amplitude, offsets):
    return pl.pallas_call(
        kernel,
        out_shape=jax.ShapeDtypeStruct((8, 2, 2, 4096), F32),
        in_specs=[pl.BlockSpec(memory_space=pl.ANY)] * 5,
        out_specs=pl.BlockSpec(memory_space=pltpu.VMEM),
        scratch_shapes=[
            pltpu.SMEM((2, 4), jnp.int32),
            pltpu.VMEM((4, 2, 256, 256), BF),
            pltpu.VMEM((2, 256, 256), F32),
            pltpu.VMEM((2, 4, 2, 256, 128), F32),
            pltpu.VMEM((3, 2, 2, 256, 128), F32),
            pltpu.VMEM((8, 4, 256, 128), F32),
            pltpu.VMEM((8, 2, 256, 128), F32),
            pltpu.VMEM((8, 2, 256, 128), F32),
            pltpu.VMEM((2, 3, 2, 256, 128), F32),
            pltpu.VMEM((2, DEVS, 3, 4, 128), F32),
            pltpu.VMEM((2, DEVS, 3, 4, 128), F32),
            pltpu.SemaphoreType.DMA((6,)),
            pltpu.SemaphoreType.DMA((8,)),
            pltpu.SemaphoreType.DMA((8,)),
            pltpu.SemaphoreType.DMA((8,)),
            pltpu.SemaphoreType.DMA((8,)),
            pltpu.SemaphoreType.DMA((2,)),
            pltpu.SemaphoreType.DMA((2,)),
            pltpu.SemaphoreType.DMA((2,)),
            pltpu.SemaphoreType.REGULAR,
        ],
        compiler_params=pltpu.CompilerParams(
            collective_id=0, has_side_effects=True, vmem_limit_bytes=VMEM_LIMIT
        ),
        name="gradient",
    )(offsets, jnp.asarray(tables()), illumination, amplitude, projection)


def solution(mesh):
    placed = (P("grp", None, None, "scan"), P(), P("grp", "scan", None, None), P("grp", "scan"))
    return jax.shard_map(
        per_device,
        mesh=mesh,
        in_specs=placed,
        out_specs=P(None, None, ("grp", "scan"), None),
        check_vma=False,
    )
```

```python
import math

import jax
import jax.numpy as jnp
import ml_dtypes
import numpy as np
from jax import lax
from jax.experimental import pallas as pl
from jax.experimental.pallas import tpu as pltpu
from jax.sharding import PartitionSpec as P

BF = jnp.bfloat16
F32 = jnp.float32
MESH = pl.DeviceIdType.MESH
GRP, SCAN = 4, 32
DEVS = GRP * SCAN
YZ = 16
ORDER = (3, 2, 1, 0)
VMEM_LIMIT = 53 << 20


def tables():
    n = np.arange(128)
    mats = []
    for odd in (0, 1):
        k = (np.arange(128) + 64 * odd) % 128
        angle = 2 * math.pi * ((n[None, :] * (2 * k[:, None] + odd)) % 256) / 256
        c, s = np.cos(angle) / 16, np.sin(angle) / 16
        forward = np.block([[c, s], [-s, c]])
        mats += [forward, forward.T]
    t = np.stack(mats)
    hi = t.astype(np.float32).astype(ml_dtypes.bfloat16)
    lo = (t - hi.astype(np.float64)).astype(np.float32).astype(ml_dtypes.bfloat16)
    return np.stack([hi, lo], 1)


def split(x):
    hi = x.astype(BF)
    return hi, (x - hi.astype(F32)).astype(BF)


def dot(a, b):
    return jnp.dot(a, b, preferred_element_type=F32)


def left(t_ref, i, x):
    hi, lo = split(x)
    return dot(t_ref[i, 0], hi) + dot(t_ref[i, 1], hi) + dot(t_ref[i, 0], lo)


def right(x, t_ref, i):
    hi, lo = split(x)
    return dot(hi, t_ref[i, 0]) + dot(lo, t_ref[i, 0]) + dot(hi, t_ref[i, 1])


def cat(xs, axis):
    return jnp.concatenate(xs, axis)


def rows_forward(tab, wr, wi):
    e = left(tab, 0, cat([wr[:128] + wr[128:], wi[:128] + wi[128:]], 0))
    o = left(tab, 2, cat([wr[:128] - wr[128:], wi[:128] - wi[128:]], 0))
    return cat([e[:128], o[:128]], 0), cat([e[128:], o[128:]], 0)


def prepare(a, j, shift, tab, ill, amp, tiles, probe, ampo, near):
    lane = lax.broadcasted_iota(jnp.int32, (256, 128), 1)
    first = lane[:128] < 64
    ia = jnp.where(first, 2 * lane[:128], 2 * lane[:128] - 127)
    ib = jnp.where(first, 2 * lane[:128] + 1, 2 * lane[:128] - 128)
    waves = []
    for p2 in range(2):
        p = 2 * j + p2
        i = a * 4 + p
        d = shift(a, p)
        turn = lax.rem(d, 128)
        for c in range(2):
            r0 = pltpu.roll(ill[c, :, 0:128], turn, 1)
            r1 = pltpu.roll(ill[c, :, 128:256], turn, 1)
            probe[i, c] = jnp.where(lane < d, r0, r1)
            probe[i, 2 + c] = jnp.where(lane < d, r1, r0)
        pr, pi = probe[i, 0], probe[i, 1]
        tr, ti = tiles[1, a, 0], tiles[1, a, 1]
        waves.append((pr * tr - pi * ti, pr * ti + pi * tr))
        for k in (0, 1):
            x = amp[a, p, 0, pl.ds(k, 128, stride=2), :]
            y = amp[a, p, 1, pl.ds(k, 128, stride=2), :]
            if k:
                x = cat([x[64:], x[:64]], 0)
                y = cat([y[64:], y[:64]], 0)
            x = jnp.take_along_axis(x, ia, axis=1, mode="promise_in_bounds")
            y = jnp.take_along_axis(y, ib, axis=1, mode="promise_in_bounds")
            ampo[i, 0, 128 * k : 128 * k + 128] = jnp.where(first, x, y)
            ampo[i, 1, 128 * k : 128 * k + 128] = jnp.where(first, y, x)
    fr, fi = rows_forward(tab, cat([waves[0][0], waves[1][0]], 1), cat([waves[0][1], waves[1][1]], 1))
    for p2 in range(2):
        i = a * 4 + 2 * j + p2
        near[i, 0] = fr[:, 128 * p2 : 128 * p2 + 128]
        near[i, 1] = fi[:, 128 * p2 : 128 * p2 + 128]


def residual(f, amp):
    re, im = f[:, :128], f[:, 128:]
    w = 1.0 - amp * lax.rsqrt(jnp.maximum(re * re + im * im, 0.25))
    return cat([re * w, im * w], 1)


def finish(a, ps, shift, tab, tiles, probe, ampo, near, acc, slot=None):
    lane = lax.broadcasted_iota(jnp.int32, (256, 128), 1)
    index = [a * 4 + p for p in ps]
    masks = [lane < shift(a, p) for p in ps]
    waves = []
    for i, m in zip(index, masks):
        pr, pi = probe[i, 2], probe[i, 3]
        if slot is None:
            tr = jnp.where(m, tiles[2, a, 0], tiles[0, a, 0])
            ti = jnp.where(m, tiles[2, a, 1], tiles[0, a, 1])
        else:
            tr, ti = tiles[slot, a, 0], tiles[slot, a, 1]
        waves.append((pr * tr - pi * ti, pr * ti + pi * tr))
    far = []
    for q in range(0, len(ps), 2):
        pair = waves[q : q + 2]
        fr, fi = rows_forward(tab, cat([w[0] for w in pair], 1), cat([w[1] for w in pair], 1))
        for u in range(len(pair)):
            far.append((fr[:, 128 * u : 128 * u + 128], fi[:, 128 * u : 128 * u + 128]))
    fields = []
    for i, (br, bi) in zip(index, far):
        ar, ai = near[i, 0], near[i, 1]
        fields.append((right(cat([ar + br, ai + bi], 1), tab, 1), right(cat([ar - br, ai - bi], 1), tab, 3)))
    backs = []
    for i, (fe, fo) in zip(index, fields):
        backs.append((right(residual(fe, ampo[i, 0]), tab, 0), right(residual(fo, ampo[i, 1]), tab, 2)))
    rows = []
    for be, bo in backs:
        lh, rh = be + bo, be - bo
        yr = cat([lh[:, :128], rh[:, :128]], 1)
        yi = cat([lh[:, 128:], rh[:, 128:]], 1)
        rows.append((left(tab, 1, cat([yr[:128], yi[:128]], 0)), left(tab, 3, cat([yr[128:], yi[128:]], 0))))
    sums = None
    for i, m, (e, o) in zip(index, masks, rows):
        top, bottom = e + o, e - o
        br = cat([top[:128], bottom[:128]], 0)
        bi = cat([top[128:], bottom[128:]], 0)
        pr, pi, qr, qi = probe[i, 0], probe[i, 1], probe[i, 2], probe[i, 3]
        gr = qr * br[:, 128:] + qi * bi[:, 128:]
        gi = qr * bi[:, 128:] - qi * br[:, 128:]
        parts = [
            jnp.where(m, 0.0, gr), jnp.where(m, 0.0, gi),
            pr * br[:, :128] + pi * bi[:, :128], pr * bi[:, :128] - pi * br[:, :128],
            jnp.where(m, gr, 0.0), jnp.where(m, gi, 0.0),
        ]
        sums = parts if sums is None else [x + y for x, y in zip(sums, parts)]
    for q in range(6):
        acc[a, q // 2, q % 2] += sums[q]


def kernel(
    off_hbm, t_hbm, ill_hbm, amp_hbm, proj_hbm, out_ref,
    off_ref, tab, ill, amp, tiles, probe, ampo, near, acc, send, recv,
    local_sem, pair_send, pair_recv, fwd_send, fwd_recv, all_send, all_recv, own_sem, ready,
):
    g, s = lax.axis_index("grp"), lax.axis_index("scan")
    me = g * SCAN + s
    yz, odd = s // 2, s % 2
    local = [
        pltpu.make_async_copy(proj_hbm, tiles.at[1], local_sem.at[0]),
        pltpu.make_async_copy(ill_hbm, ill, local_sem.at[1]),
        pltpu.make_async_copy(t_hbm, tab, local_sem.at[2]),
        pltpu.make_async_copy(amp_hbm.at[:, :, :, pl.ds(0, 128)], amp.at[:, :, 0], local_sem.at[3]),
        pltpu.make_async_copy(amp_hbm.at[:, :, :, pl.ds(128, 128)], amp.at[:, :, 1], local_sem.at[4]),
        pltpu.make_async_copy(off_hbm, off_ref, local_sem.at[5]),
    ]
    barrier = pltpu.get_barrier_semaphore()
    row = g * 2 + odd
    for k in range(1, 8):
        other = (row + k) % 8
        pl.semaphore_signal(
            barrier, inc=1, device_id={"grp": other // 2, "scan": yz * 2 + other % 2}, device_id_type=MESH
        )
    for k in range(1, YZ):
        pl.semaphore_signal(
            barrier, inc=1, device_id={"grp": g, "scan": (yz + k) % YZ * 2 + odd}, device_id_type=MESH
        )
    for c in local:
        c.start()
    acc[...] = jnp.zeros_like(acc)
    sends_on = jnp.logical_and(s != SCAN - 2, s != 1)
    gets = jnp.logical_and(s != 0, s != SCAN - 1)

    @pl.when(jnp.logical_not(gets))
    def _():
        tiles[2 * odd] = jnp.zeros_like(tiles[0])

    pl.semaphore_wait(barrier, 7 + YZ - 1)

    near_slot = 2 - 2 * odd
    chunks = [(a, c, h) for a in range(2) for c in range(2) for h in range(2)]

    def pair_copy(i):
        a, c, h = chunks[i]
        rows = pl.ds(128 * h, 128)
        return pltpu.make_async_remote_copy(
            proj_hbm.at[a, c, rows], tiles.at[2 * odd, a, c, rows], pair_send.at[i], pair_recv.at[i],
            device_id={"grp": g, "scan": s + 1 - 2 * odd}, device_id_type=MESH,
        )

    def fwd_copy(i):
        a, c, h = chunks[i]
        rows = pl.ds(128 * h, 128)
        return pltpu.make_async_remote_copy(
            tiles.at[near_slot, a, c, rows], tiles.at[2 * odd, a, c, rows], fwd_send.at[i], fwd_recv.at[i],
            device_id={"grp": g, "scan": s + 2 - 4 * odd}, device_id_type=MESH,
        )

    def pass_on(i):
        pair_copy(i).wait_recv()

        @pl.when(sends_on)
        def _():
            fwd_copy(i).start()

    def all_copy(a, k):
        to = (me + k) % DEVS
        return pltpu.make_async_remote_copy(
            send.at[a, to], recv.at[a, me], all_send.at[a], all_recv.at[a, g],
            device_id={"grp": to // SCAN, "scan": to % SCAN}, device_id_type=MESH,
        )

    def shift(a, p):
        return off_ref[a, p] - (s * 128 - 128)

    for i in range(4):
        pair_copy(i).start()
    for k in range(1, YZ):
        pl.semaphore_signal(
            ready, inc=1, device_id={"grp": g, "scan": (yz + k) % YZ * 2 + odd}, device_id_type=MESH
        )
    for c in local:
        c.wait()
    for q in range(4):
        prepare(q // 2, q % 2, shift, tab, ill, amp, tiles, probe, ampo, near)
        pass_on(q)
        pair_copy(q).wait_send()
        pair_copy(q + 4).start()

    soon = 1 - odd
    later = [odd, 2, 3]

    def forwarded(a):
        @pl.when(gets)
        def _():
            for i in range(4 * a, 4 * a + 4):
                fwd_copy(i).wait_recv()

    for a in range(2):
        if a == 0:
            finish(a, [soon], shift, tab, tiles, probe, ampo, near, acc, near_slot)
            pass_on(4)
            pass_on(5)
            pass_on(6)
            forwarded(0)
            finish(a, later, shift, tab, tiles, probe, ampo, near, acc)
            pass_on(7)
        else:
            forwarded(1)
            finish(a, [0, 1, 2, 3], shift, tab, tiles, probe, ampo, near, acc)

        def pack(q, carry):
            for u in range(4):
                to = q * 4 + u
                for t in range(3):
                    for c in range(2):
                        send[a, to, t, 2 * c : 2 * c + 2, :] = acc[a, t, c, pl.ds(to * 2, 2), :]
            return carry

        lax.fori_loop(0, DEVS // 4, pack, 0)
        if a == 0:
            pl.semaphore_wait(ready, YZ - 1)

        def post(k, carry):
            all_copy(a, k).start()
            return carry

        lax.fori_loop(1, DEVS, post, 0)
        pltpu.make_async_copy(send.at[a, me], recv.at[a, me], own_sem.at[a]).start()

    for i in range(8):
        if i >= 4:
            pair_copy(i).wait_send()

        @pl.when(sends_on)
        def _():
            fwd_copy(i).wait_send()

    for a in range(2):
        pltpu.make_async_copy(send.at[a, me], recv.at[a, me], own_sem.at[a]).wait()

        def bulk(n, h):
            return pltpu.make_async_remote_copy(
                send.at[a, pl.ds(0, n)], recv.at[a, pl.ds(0, n)], all_send.at[a], all_recv.at[a, h],
                device_id={"grp": g, "scan": s + 1 - 2 * odd}, device_id_type=MESH,
            )

        def gather(h):
            for t in range(SCAN):
                total = None
                for k in range(3):
                    src = t + 1 - k
                    if 0 <= src < SCAN:
                        x = recv[a, h * SCAN + src, k]
                        total = x if total is None else total + x
                for c in range(2):
                    out_ref[2 * h + a, c, :, 128 * t : 128 * t + 128] = total[2 * c : 2 * c + 2]

        for k in ORDER:
            h = (g + k) % GRP
            bulk(SCAN if k else SCAN - 1, h).wait_recv()
            gather(h)
        bulk(DEVS - 1, g).wait_send()


def per_device(projection, illumination, amplitude, offsets):
    return pl.pallas_call(
        kernel,
        out_shape=jax.ShapeDtypeStruct((8, 2, 2, 4096), F32),
        in_specs=[pl.BlockSpec(memory_space=pl.ANY)] * 5,
        out_specs=pl.BlockSpec(memory_space=pltpu.VMEM),
        scratch_shapes=[
            pltpu.SMEM((2, 4), jnp.int32),
            pltpu.VMEM((4, 2, 256, 256), BF),
            pltpu.VMEM((2, 256, 256), F32),
            pltpu.VMEM((2, 4, 2, 256, 128), F32),
            pltpu.VMEM((3, 2, 2, 256, 128), F32),
            pltpu.VMEM((8, 4, 256, 128), F32),
            pltpu.VMEM((8, 2, 256, 128), F32),
            pltpu.VMEM((8, 2, 256, 128), F32),
            pltpu.VMEM((2, 3, 2, 256, 128), F32),
            pltpu.VMEM((2, DEVS, 3, 4, 128), F32),
            pltpu.VMEM((2, DEVS, 3, 4, 128), F32),
            pltpu.SemaphoreType.DMA((6,)),
            pltpu.SemaphoreType.DMA((8,)),
            pltpu.SemaphoreType.DMA((8,)),
            pltpu.SemaphoreType.DMA((8,)),
            pltpu.SemaphoreType.DMA((8,)),
            pltpu.SemaphoreType.DMA((2,)),
            pltpu.SemaphoreType.DMA((2, GRP)),
            pltpu.SemaphoreType.DMA((2,)),
            pltpu.SemaphoreType.REGULAR,
        ],
        compiler_params=pltpu.CompilerParams(
            collective_id=0, has_side_effects=True, vmem_limit_bytes=VMEM_LIMIT
        ),
        name="gradient",
    )(offsets, jnp.asarray(tables()), illumination, amplitude, projection)


def solution(mesh):
    placed = (P("grp", None, None, "scan"), P(), P("grp", "scan", None, None), P("grp", "scan"))
    return jax.shard_map(
        per_device,
        mesh=mesh,
        in_specs=placed,
        out_specs=P(None, None, ("grp", "scan"), None),
        check_vma=False,
    )
```

```python
import math

import jax
import jax.numpy as jnp
import ml_dtypes
import numpy as np
from jax import lax
from jax.experimental import pallas as pl
from jax.experimental.pallas import tpu as pltpu
from jax.sharding import PartitionSpec as P

BF = jnp.bfloat16
F32 = jnp.float32
MESH = pl.DeviceIdType.MESH
GRP, SCAN = 4, 32
DEVS = GRP * SCAN
YZ = 16
BATCH = 8
ORDER = (3, 2, 1, 0)
VMEM_LIMIT = 53 << 20


def tables():
    n = np.arange(128)
    mats = []
    for odd in (0, 1):
        k = (np.arange(128) + 64 * odd) % 128
        angle = 2 * math.pi * ((n[None, :] * (2 * k[:, None] + odd)) % 256) / 256
        c, s = np.cos(angle) / 16, np.sin(angle) / 16
        forward = np.block([[c, s], [-s, c]])
        mats += [forward, forward.T]
    t = np.stack(mats)
    hi = t.astype(np.float32).astype(ml_dtypes.bfloat16)
    lo = (t - hi.astype(np.float64)).astype(np.float32).astype(ml_dtypes.bfloat16)
    return np.stack([hi, lo], 1)


def split(x):
    hi = x.astype(BF)
    return hi, (x - hi.astype(F32)).astype(BF)


def dot(a, b):
    return jnp.dot(a, b, preferred_element_type=F32)


def left(t_ref, i, x):
    hi, lo = split(x)
    return dot(t_ref[i, 0], hi) + dot(t_ref[i, 1], hi) + dot(t_ref[i, 0], lo)


def right(x, t_ref, i):
    hi, lo = split(x)
    return dot(hi, t_ref[i, 0]) + dot(lo, t_ref[i, 0]) + dot(hi, t_ref[i, 1])


def cat(xs, axis):
    return jnp.concatenate(xs, axis)


def rows_forward(tab, wr, wi):
    e = left(tab, 0, cat([wr[:128] + wr[128:], wi[:128] + wi[128:]], 0))
    o = left(tab, 2, cat([wr[:128] - wr[128:], wi[:128] - wi[128:]], 0))
    return cat([e[:128], o[:128]], 0), cat([e[128:], o[128:]], 0)


def prepare(a, j, shift, tab, ill, amp, tiles, probe, ampo, near):
    lane = lax.broadcasted_iota(jnp.int32, (256, 128), 1)
    first = lane[:128] < 64
    ia = jnp.where(first, 2 * lane[:128], 2 * lane[:128] - 127)
    ib = jnp.where(first, 2 * lane[:128] + 1, 2 * lane[:128] - 128)
    waves = []
    for p2 in range(2):
        p = 2 * j + p2
        i = a * 4 + p
        d = shift(a, p)
        turn = lax.rem(d, 128)
        for c in range(2):
            r0 = pltpu.roll(ill[c, :, 0:128], turn, 1)
            r1 = pltpu.roll(ill[c, :, 128:256], turn, 1)
            probe[i, c] = jnp.where(lane < d, r0, r1)
            probe[i, 2 + c] = jnp.where(lane < d, r1, r0)
        pr, pi = probe[i, 0], probe[i, 1]
        tr, ti = tiles[1, a, 0], tiles[1, a, 1]
        waves.append((pr * tr - pi * ti, pr * ti + pi * tr))
        for k in (0, 1):
            x = amp[a, p, 0, pl.ds(k, 128, stride=2), :]
            y = amp[a, p, 1, pl.ds(k, 128, stride=2), :]
            if k:
                x = cat([x[64:], x[:64]], 0)
                y = cat([y[64:], y[:64]], 0)
            x = jnp.take_along_axis(x, ia, axis=1, mode="promise_in_bounds")
            y = jnp.take_along_axis(y, ib, axis=1, mode="promise_in_bounds")
            ampo[i, 0, 128 * k : 128 * k + 128] = jnp.where(first, x, y)
            ampo[i, 1, 128 * k : 128 * k + 128] = jnp.where(first, y, x)
    fr, fi = rows_forward(tab, cat([waves[0][0], waves[1][0]], 1), cat([waves[0][1], waves[1][1]], 1))
    for p2 in range(2):
        i = a * 4 + 2 * j + p2
        near[i, 0] = fr[:, 128 * p2 : 128 * p2 + 128]
        near[i, 1] = fi[:, 128 * p2 : 128 * p2 + 128]


def residual(f, amp):
    re, im = f[:, :128], f[:, 128:]
    w = 1.0 - amp * lax.rsqrt(jnp.maximum(re * re + im * im, 0.25))
    return cat([re * w, im * w], 1)


def finish(a, ps, shift, tab, tiles, probe, ampo, near, acc, slot=None):
    lane = lax.broadcasted_iota(jnp.int32, (256, 128), 1)
    index = [a * 4 + p for p in ps]
    masks = [lane < shift(a, p) for p in ps]
    waves = []
    for i, m in zip(index, masks):
        pr, pi = probe[i, 2], probe[i, 3]
        if slot is None:
            tr = jnp.where(m, tiles[2, a, 0], tiles[0, a, 0])
            ti = jnp.where(m, tiles[2, a, 1], tiles[0, a, 1])
        else:
            tr, ti = tiles[slot, a, 0], tiles[slot, a, 1]
        waves.append((pr * tr - pi * ti, pr * ti + pi * tr))
    far = []
    for q in range(0, len(ps), 2):
        pair = waves[q : q + 2]
        fr, fi = rows_forward(tab, cat([w[0] for w in pair], 1), cat([w[1] for w in pair], 1))
        for u in range(len(pair)):
            far.append((fr[:, 128 * u : 128 * u + 128], fi[:, 128 * u : 128 * u + 128]))
    fields = []
    for i, (br, bi) in zip(index, far):
        ar, ai = near[i, 0], near[i, 1]
        fields.append((right(cat([ar + br, ai + bi], 1), tab, 1), right(cat([ar - br, ai - bi], 1), tab, 3)))
    backs = []
    for i, (fe, fo) in zip(index, fields):
        backs.append((right(residual(fe, ampo[i, 0]), tab, 0), right(residual(fo, ampo[i, 1]), tab, 2)))
    rows = []
    for be, bo in backs:
        lh, rh = be + bo, be - bo
        yr = cat([lh[:, :128], rh[:, :128]], 1)
        yi = cat([lh[:, 128:], rh[:, 128:]], 1)
        rows.append((left(tab, 1, cat([yr[:128], yi[:128]], 0)), left(tab, 3, cat([yr[128:], yi[128:]], 0))))
    sums = None
    for i, m, (e, o) in zip(index, masks, rows):
        top, bottom = e + o, e - o
        br = cat([top[:128], bottom[:128]], 0)
        bi = cat([top[128:], bottom[128:]], 0)
        pr, pi, qr, qi = probe[i, 0], probe[i, 1], probe[i, 2], probe[i, 3]
        gr = qr * br[:, 128:] + qi * bi[:, 128:]
        gi = qr * bi[:, 128:] - qi * br[:, 128:]
        parts = [
            jnp.where(m, 0.0, gr), jnp.where(m, 0.0, gi),
            pr * br[:, :128] + pi * bi[:, :128], pr * bi[:, :128] - pi * br[:, :128],
            jnp.where(m, gr, 0.0), jnp.where(m, gi, 0.0),
        ]
        sums = parts if sums is None else [x + y for x, y in zip(sums, parts)]
    for q in range(6):
        acc[a, q // 2, q % 2] += sums[q]


def kernel(
    off_hbm, t_hbm, ill_hbm, amp_hbm, proj_hbm, out_ref,
    off_ref, tab, ill, amp, tiles, probe, ampo, near, acc, send, recv,
    local_sem, pair_send, pair_recv, fwd_send, fwd_recv, all_send, all_recv, own_sem, ready,
):
    g, s = lax.axis_index("grp"), lax.axis_index("scan")
    me = g * SCAN + s
    yz, odd = s // 2, s % 2
    local = [
        pltpu.make_async_copy(proj_hbm, tiles.at[1], local_sem.at[0]),
        pltpu.make_async_copy(ill_hbm, ill, local_sem.at[1]),
        pltpu.make_async_copy(t_hbm, tab, local_sem.at[2]),
        pltpu.make_async_copy(amp_hbm.at[:, :, :, pl.ds(0, 128)], amp.at[:, :, 0], local_sem.at[3]),
        pltpu.make_async_copy(amp_hbm.at[:, :, :, pl.ds(128, 128)], amp.at[:, :, 1], local_sem.at[4]),
        pltpu.make_async_copy(off_hbm, off_ref, local_sem.at[5]),
    ]
    barrier = pltpu.get_barrier_semaphore()
    row = g * 2 + odd
    for k in range(1, 8):
        other = (row + k) % 8
        pl.semaphore_signal(
            barrier, inc=1, device_id={"grp": other // 2, "scan": yz * 2 + other % 2}, device_id_type=MESH
        )
    for k in range(1, YZ):
        pl.semaphore_signal(
            barrier, inc=1, device_id={"grp": g, "scan": (yz + k) % YZ * 2 + odd}, device_id_type=MESH
        )
    for c in local:
        c.start()
    acc[...] = jnp.zeros_like(acc)
    sends_on = jnp.logical_and(s != SCAN - 2, s != 1)
    gets = jnp.logical_and(s != 0, s != SCAN - 1)

    @pl.when(jnp.logical_not(gets))
    def _():
        tiles[2 * odd] = jnp.zeros_like(tiles[0])

    pl.semaphore_wait(barrier, 7 + YZ - 1)

    near_slot = 2 - 2 * odd
    chunks = [(a, c, h) for a in range(2) for c in range(2) for h in range(2)]

    def pair_copy(i):
        a, c, h = chunks[i]
        rows = pl.ds(128 * h, 128)
        return pltpu.make_async_remote_copy(
            proj_hbm.at[a, c, rows], tiles.at[2 * odd, a, c, rows], pair_send.at[i], pair_recv.at[i],
            device_id={"grp": g, "scan": s + 1 - 2 * odd}, device_id_type=MESH,
        )

    def fwd_copy(i):
        a, c, h = chunks[i]
        rows = pl.ds(128 * h, 128)
        return pltpu.make_async_remote_copy(
            tiles.at[near_slot, a, c, rows], tiles.at[2 * odd, a, c, rows], fwd_send.at[i], fwd_recv.at[i],
            device_id={"grp": g, "scan": s + 2 - 4 * odd}, device_id_type=MESH,
        )

    def pass_on(i):
        pair_copy(i).wait_recv()

        @pl.when(sends_on)
        def _():
            fwd_copy(i).start()

    def all_copy(a, k):
        to = (me + k) % DEVS
        return pltpu.make_async_remote_copy(
            send.at[a, to], recv.at[a, me], all_send.at[a], all_recv.at[a, g],
            device_id={"grp": to // SCAN, "scan": to % SCAN}, device_id_type=MESH,
        )

    def shift(a, p):
        return off_ref[a, p] - (s * 128 - 128)

    for i in range(4):
        pair_copy(i).start()
    for k in range(1, YZ):
        pl.semaphore_signal(
            ready, inc=1, device_id={"grp": g, "scan": (yz + k) % YZ * 2 + odd}, device_id_type=MESH
        )
    for c in local:
        c.wait()
    for q in range(4):
        prepare(q // 2, q % 2, shift, tab, ill, amp, tiles, probe, ampo, near)
        pass_on(q)
        pair_copy(q).wait_send()
        pair_copy(q + 4).start()

    soon = 1 - odd
    later = [odd, 2, 3]

    def forwarded(a):
        @pl.when(gets)
        def _():
            for i in range(4 * a, 4 * a + 4):
                fwd_copy(i).wait_recv()

    for a in range(2):
        if a == 0:
            finish(a, [soon], shift, tab, tiles, probe, ampo, near, acc, near_slot)
            pass_on(4)
            pass_on(5)
            pass_on(6)
            forwarded(0)
            finish(a, later, shift, tab, tiles, probe, ampo, near, acc)
            pass_on(7)
        else:
            finish(a, [soon], shift, tab, tiles, probe, ampo, near, acc, near_slot)
            forwarded(1)
            finish(a, later, shift, tab, tiles, probe, ampo, near, acc)

        def pack(to):
            for t in range(3):
                for c in range(2):
                    send[a, to, t, 2 * c : 2 * c + 2, :] = acc[a, t, c, pl.ds(to * 2, 2), :]

        if a == 0:
            pl.semaphore_wait(ready, YZ - 1)

        def post(first, count):
            for k in range(count):
                pack((me + first + k) % DEVS)
            for k in range(count):
                all_copy(a, first + k).start()

        def posts(q, carry):
            post(q * BATCH + 1, BATCH)
            return carry

        lax.fori_loop(0, (DEVS - 1) // BATCH, posts, 0)
        post((DEVS - 1) // BATCH * BATCH + 1, (DEVS - 1) % BATCH)
        pack(me)
        pltpu.make_async_copy(send.at[a, me], recv.at[a, me], own_sem.at[a]).start()

    for i in range(8):
        if i >= 4:
            pair_copy(i).wait_send()

        @pl.when(sends_on)
        def _():
            fwd_copy(i).wait_send()

    for a in range(2):
        pltpu.make_async_copy(send.at[a, me], recv.at[a, me], own_sem.at[a]).wait()

        def bulk(n, h):
            return pltpu.make_async_remote_copy(
                send.at[a, pl.ds(0, n)], recv.at[a, pl.ds(0, n)], all_send.at[a], all_recv.at[a, h],
                device_id={"grp": g, "scan": s + 1 - 2 * odd}, device_id_type=MESH,
            )

        def gather(h):
            for t in range(SCAN):
                total = None
                for k in range(3):
                    src = t + 1 - k
                    if 0 <= src < SCAN:
                        x = recv[a, h * SCAN + src, k]
                        total = x if total is None else total + x
                for c in range(2):
                    out_ref[2 * h + a, c, :, 128 * t : 128 * t + 128] = total[2 * c : 2 * c + 2]

        for k in ORDER:
            h = (g + k) % GRP
            bulk(SCAN if k else SCAN - 1, h).wait_recv()
            gather(h)
        bulk(DEVS - 1, g).wait_send()


def per_device(projection, illumination, amplitude, offsets):
    return pl.pallas_call(
        kernel,
        out_shape=jax.ShapeDtypeStruct((8, 2, 2, 4096), F32),
        in_specs=[pl.BlockSpec(memory_space=pl.ANY)] * 5,
        out_specs=pl.BlockSpec(memory_space=pltpu.VMEM),
        scratch_shapes=[
            pltpu.SMEM((2, 4), jnp.int32),
            pltpu.VMEM((4, 2, 256, 256), BF),
            pltpu.VMEM((2, 256, 256), F32),
            pltpu.VMEM((2, 4, 2, 256, 128), F32),
            pltpu.VMEM((3, 2, 2, 256, 128), F32),
            pltpu.VMEM((8, 4, 256, 128), F32),
            pltpu.VMEM((8, 2, 256, 128), F32),
            pltpu.VMEM((8, 2, 256, 128), F32),
            pltpu.VMEM((2, 3, 2, 256, 128), F32),
            pltpu.VMEM((2, DEVS, 3, 4, 128), F32),
            pltpu.VMEM((2, DEVS, 3, 4, 128), F32),
            pltpu.SemaphoreType.DMA((6,)),
            pltpu.SemaphoreType.DMA((8,)),
            pltpu.SemaphoreType.DMA((8,)),
            pltpu.SemaphoreType.DMA((8,)),
            pltpu.SemaphoreType.DMA((8,)),
            pltpu.SemaphoreType.DMA((2,)),
            pltpu.SemaphoreType.DMA((2, GRP)),
            pltpu.SemaphoreType.DMA((2,)),
            pltpu.SemaphoreType.REGULAR,
        ],
        compiler_params=pltpu.CompilerParams(
            collective_id=0, has_side_effects=True, vmem_limit_bytes=VMEM_LIMIT
        ),
        name="gradient",
    )(offsets, jnp.asarray(tables()), illumination, amplitude, projection)


def solution(mesh):
    placed = (P("grp", None, None, "scan"), P(), P("grp", "scan", None, None), P("grp", "scan"))
    return jax.shard_map(
        per_device,
        mesh=mesh,
        in_specs=placed,
        out_specs=P(None, None, ("grp", "scan"), None),
        check_vma=False,
    )
```
